256 devices in a mesh: tm: 8 (over z), chan: 32 (over y, x, core).
Axes of the slice: x: 4, y: 4, z: 8, core: 2. Of those that a mesh axis runs over, the one named last changes fastest.
Arguments:
- raw: bfloat16 [12288, 16384], P(('tm', 'chan')), may hold values from -6 to 6
- band_taps: bfloat16 [128], replicated, may hold values from -0.5 to 0.5
- real_taps: bfloat16 [128], replicated, may hold values from -0.5 to 0.5
- imag_taps: bfloat16 [128], replicated, may hold values from -0.5 to 0.5
- short_taps: bfloat16 [128], replicated, may hold values from 0.0039978027 to 0.011962891
- lta_rate: float32 [16384], P('chan'), may hold values from 1.6276042e-06 to 0.03125
- lta_start: float32 [16384], P('chan'), may hold values from 0.5 to 4
- gap_gain: float32 [12288], P('tm'), may hold values from 0.5 to 1
Outputs:
- ratio: float32 [12288, 16384], P('tm', 'chan')
The draws below stay inside these ranges and needn't reach their ends.
All inputs are finite; a program needn't handle non-finite values.
Results may differ from the reference program's by a relative error of at most 0.00091.
Values may be sent and summed in bfloat16 or wider, within the bound.
No kernel may reach another device: no remote copies, remote signals or barrier semaphores. Data moves between devices by JAX's collectives and lax.ppermute only.
A program may use at most 64 MiB of HBM per device.

```python
import math
import jax
import jax.numpy as jnp
from jax import lax

BLOCK = 128
CH_DEV = 512
TIMES = 12288
CHANNELS = 16384


def draw_lta_rate(key, part):
    key = jax.random.fold_in(key, 11)
    low = jnp.log(0.02 / TIMES)
    high = jnp.log(0.03125)
    uniform_a = jax.random.uniform(jax.random.fold_in(key, 1), (CHANNELS,), jnp.float32)
    return jnp.exp(low + (high - low) * uniform_a).astype(jnp.float32)


def draw_gap_gain(key, part):
    key = jax.random.fold_in(key, 23)
    places = jax.random.randint(jax.random.fold_in(key, 1), (4,), 0, TIMES)
    levels = jax.random.uniform(jax.random.fold_in(key, 2), (4,), jnp.float32, 0.5, 0.8)
    moments = jnp.arange(TIMES)
    hits = moments[:, None] == places[None, :]
    return jnp.prod(jnp.where(hits, levels[None, :], 1.0), axis=1).astype(jnp.float32)


def shard_levels(stream_key, dims, shards, least, top_value):
    gain = 1.0
    for axis_at, blocks in shards:
        steps = jax.random.uniform(jax.random.fold_in(jax.random.fold_in(stream_key, 6), axis_at), (blocks,), jnp.float32, least / len(shards), top_value / len(shards))
        gain = gain * jnp.repeat(jnp.exp(steps), dims[axis_at] // blocks).reshape((-1,) + (1,) * (len(dims) - 1 - axis_at))
    return gain


def normal_values(own_key, extent, spread, reach, split=(), held_as=jnp.bfloat16):
    loudness = shard_levels(own_key, extent, split, -0.22, 0.18) if split else 1.0
    result = jax.random.normal(own_key, extent, jnp.float32) * spread * loudness
    return jnp.minimum(jnp.maximum(result, -reach), reach).astype(held_as)


def setup_inputs(seed: int = 0) -> dict:
    keys = jax.random.split(jax.random.key(seed), 9)
    raw = normal_values(keys[0], (TIMES, CHANNELS), 1.0, 6.0, ((0, 256),))
    band_taps = normal_values(keys[1], (BLOCK,), BLOCK ** -0.5, 0.5)
    real_taps = normal_values(keys[2], (BLOCK,), BLOCK ** -0.5, 0.5)
    imag_taps = normal_values(keys[3], (BLOCK,), BLOCK ** -0.5, 0.5)
    short_taps = jnp.clip(jax.random.uniform(keys[4], (BLOCK,), jnp.float32, 0.0039978027, 0.011962891), 0.0039978027, 0.011962891).astype(jnp.bfloat16)
    lta_rate = draw_lta_rate(jax.random.fold_in(keys[8], 71), 0)
    lta_start = jnp.clip(jnp.exp(math.log(4.0) - 2.0794415 * jax.random.uniform(keys[6], (CHANNELS,), jnp.float32) ** shard_levels(keys[6], (CHANNELS,), ((0, 32),), -0.2, 0.2)), 0.5, 4.0)
    gap_gain = draw_gap_gain(jax.random.fold_in(keys[8], 71), 0)
    return {"raw": raw, "band_taps": band_taps, "real_taps": real_taps, "imag_taps": imag_taps, "short_taps": short_taps, "lta_rate": lta_rate, "lta_start": lta_start, "gap_gain": gap_gain}


def band_matrices(taps):
    lag = jnp.arange(BLOCK)[:, None] - jnp.arange(BLOCK)[None, :]
    picks = jnp.arange(BLOCK)
    weights = taps.astype(jnp.float32)
    current = jnp.sum(jnp.where(lag[:, :, None] == picks[None, None, :], weights, 0.0), axis=2)
    earlier = jnp.sum(jnp.where((lag + BLOCK)[:, :, None] == picks[None, None, :], weights, 0.0), axis=2)
    return current, earlier


def block_filter(signal, taps, history):
    current, earlier = band_matrices(taps)
    rows, cols = signal.shape
    blocks = signal.astype(jnp.float32).reshape(rows // BLOCK, BLOCK, cols)
    prior = jnp.concatenate([history.astype(jnp.float32)[None], blocks[:-1]], axis=0)
    out = jnp.einsum("ij,bjc->bic", current, blocks) + jnp.einsum("ij,bjc->bic", earlier, prior)
    return out.reshape(rows, cols)


def reference(raw, band_taps, real_taps, imag_taps, short_taps, lta_rate, lta_start, gap_gain):
    groups = CHANNELS // CH_DEV
    columns = raw.reshape(TIMES, groups, CH_DEV).transpose(1, 0, 2)
    rates = lta_rate.reshape(groups, CH_DEV)
    starts = lta_start.reshape(groups, CH_DEV)

    def one_group(inputs):
        raw_cols, rate, start = inputs
        zeros = jnp.zeros((BLOCK, CH_DEV), jnp.float32)
        band = block_filter(raw_cols, band_taps, zeros).astype(jnp.bfloat16)
        real_part = block_filter(band, real_taps, zeros)
        imag_part = block_filter(band, imag_taps, zeros)
        energy = (real_part * real_part + imag_part * imag_part).astype(jnp.bfloat16)
        short = block_filter(energy, short_taps, zeros)
        keep = 1.0 - rate

        def advance(state, inputs_row):
            sample_gain, energy_row = inputs_row
            state = keep * sample_gain * state + rate * energy_row.astype(jnp.float32)
            return state, state

        final, long_avg = lax.scan(advance, start, (gap_gain, energy))
        return short / long_avg

    ratios = lax.map(one_group, (columns, rates, starts))
    return ratios.transpose(1, 0, 2).reshape(TIMES, CHANNELS)
```

```python
import functools

import jax
import jax.numpy as jnp
from jax import lax
from jax.experimental import pallas as pl
from jax.experimental.pallas import tpu as pltpu
from jax.sharding import PartitionSpec as P

BLOCK = 128
SUB = 64
VMEM = pl.BlockSpec(memory_space=pltpu.VMEM)
SMEM = pl.BlockSpec(memory_space=pltpu.SMEM)


def dot(a, b):
    return jnp.dot(a, b, preferred_element_type=jnp.float32)


def call(kernel, out_shape, in_specs, out_specs=None, scratch=(), limit=24):
    if out_specs is None:
        out_specs = jax.tree.map(lambda _: VMEM, out_shape)
    return pl.pallas_call(
        kernel,
        out_shape=out_shape,
        in_specs=in_specs,
        out_specs=out_specs,
        scratch_shapes=scratch,
        compiler_params=pltpu.CompilerParams(vmem_limit_bytes=limit * 1024 * 1024),
    )


def from_behind(value, axis):
    count = lax.axis_size(axis)
    return lax.ppermute(value, axis, [(source, source + 1) for source in range(count - 1)])


def matrices_kernel(rows_ref, band_ref, pair_ref, short_ref, sums_ref):
    def toeplitz(k):
        row = jnp.broadcast_to(rows_ref[k : k + 1, :], (BLOCK, 2 * BLOCK))
        return pltpu.roll(row, 0, 1, stride=1, stride_axis=0).astype(jnp.bfloat16)

    band_ref[...] = toeplitz(0)
    pair_ref[:BLOCK, :] = toeplitz(1)
    pair_ref[BLOCK:, :] = toeplitz(2)
    short_ref[...] = toeplitz(3)
    row = lax.broadcasted_iota(jnp.int32, (BLOCK, 2 * BLOCK), 0)
    col = lax.broadcasted_iota(jnp.int32, (BLOCK, 2 * BLOCK), 1) % BLOCK
    keep = (col <= row) & (col // SUB == row // SUB)
    sums_ref[...] = jnp.where(keep, 1.0, 0.0).astype(jnp.bfloat16)


def energy_of(pair, window):
    both = dot(pair, window)
    real, imag = both[:BLOCK], both[BLOCK:]
    return (real * real + imag * imag).astype(jnp.bfloat16)


def lanes(column, cols):
    return jnp.concatenate([column] * (cols // 128), axis=1)


def running_of(energy, sums, rate_scale, gain_scale):
    cols = energy.shape[1]
    scaled = energy.astype(jnp.float32) * rate_scale * lanes(gain_scale, cols)
    high = scaled.astype(jnp.bfloat16)
    low = (scaled - high.astype(jnp.float32)).astype(jnp.bfloat16)
    return dot(sums, jnp.concatenate([high, low], axis=0))


def short_of(short, window, scale, gain_scale):
    return dot(short, window) * scale * lanes(gain_scale, window.shape[1])


def main_kernel(
    count, signal, band_m, pair_m, short_m, sums_m, rate_scale, scale, gain_scale,
    band1, energy2, energy_last, running, upper, band, energy,
):
    def rows(b, n=1):
        return pl.ds(pl.multiple_of(b * BLOCK, BLOCK), n * BLOCK)

    def band_step(b, _):
        band[rows(b), :] = dot(band_m[...], signal[rows(b - 1, 2), :]).astype(jnp.bfloat16)
        return 0

    lax.fori_loop(1, count, band_step, 0, unroll=True)

    def energy_step(b, _):
        e = energy_of(pair_m[...], band[rows(b - 1, 2), :])
        energy[rows(b), :] = e
        running[rows(b - 2), :] = running_of(e, sums_m[...], rate_scale[...], gain_scale[rows(b), :])
        return 0

    lax.fori_loop(2, count, energy_step, 0, unroll=True)

    def short_step(b, _):
        upper[rows(b - 3), :] = short_of(
            short_m[...], energy[rows(b - 1, 2), :], scale[...], gain_scale[rows(b), :]
        )
        return 0

    lax.fori_loop(3, count, short_step, 0, unroll=True)
    band1[...] = band[rows(1), :]
    energy2[...] = energy[rows(2), :]
    energy_last[...] = energy[rows(count - 1), :]


def edge_kernel(
    subs, prior, signal, band1, energy2, running, band_m, pair_m, short_m, sums_m,
    rate_scale, scale, gain_scale, ends,
    energy0, running01, upper12, totals,
):
    h1 = prior[BLOCK:, :]
    band_before = dot(band_m[...], prior[...]).astype(jnp.bfloat16)
    band0 = dot(band_m[...], jnp.concatenate([h1, signal[:BLOCK, :]], axis=0)).astype(jnp.bfloat16)
    e0 = energy_of(pair_m[...], jnp.concatenate([band_before, band0], axis=0))
    e1 = energy_of(pair_m[...], jnp.concatenate([band0, band1[...]], axis=0))
    energy0[...] = e0
    run0 = running_of(e0, sums_m[...], rate_scale[...], gain_scale[:BLOCK, :])
    run1 = running_of(e1, sums_m[...], rate_scale[...], gain_scale[BLOCK : 2 * BLOCK, :])
    running01[:BLOCK, :] = run0
    running01[BLOCK:, :] = run1
    upper12[:BLOCK, :] = short_of(
        short_m[...], jnp.concatenate([e0, e1], axis=0), scale[...], gain_scale[BLOCK : 2 * BLOCK, :]
    )
    upper12[BLOCK:, :] = short_of(
        short_m[...],
        jnp.concatenate([e1, energy2[...]], axis=0),
        scale[...],
        gain_scale[2 * BLOCK : 3 * BLOCK, :],
    )
    first = (run0, run1)
    value = jnp.zeros_like(ends[0:1, :])
    decay = jnp.ones_like(value)
    for s in range(subs):
        last = (s % 2) * SUB + SUB - 1
        if s < 4:
            end = first[s // 2][last : last + 1, :]
        else:
            end = running[s * SUB - 2 * BLOCK + SUB - 1 : s * SUB - 2 * BLOCK + SUB, :]
        step = ends[s : s + 1, :]
        value = step * (value + end)
        decay = decay * step
    both = jnp.concatenate([decay, value], axis=0)
    for k in range(totals.shape[0]):
        totals[k] = both


def ratio_kernel(
    subs, chunks, position, totals, start, energy_before, energy0, running01, running, upper12, upper,
    short_m, scale, gain_scale, ends, out, buffer, sems,
):
    state = start[...]
    for k in range(totals.shape[0]):
        new = totals[k, 0:1, :] * state + totals[k, 1:2, :]
        state = jnp.where(k < position[0], new, state)
    upper0 = short_of(
        short_m[...],
        jnp.concatenate([energy_before[...], energy0[...]], axis=0),
        scale[...],
        gain_scale[:BLOCK, :],
    )
    rows = subs * SUB // chunks
    copies = []
    for s in range(subs):
        at = s * SUB
        if at < 2 * BLOCK:
            run = running01[at : at + SUB, :]
        else:
            run = running[at - 2 * BLOCK : at - 2 * BLOCK + SUB, :]
        if at < BLOCK:
            top = upper0[at : at + SUB, :]
        elif at < 3 * BLOCK:
            top = upper12[at - BLOCK : at - BLOCK + SUB, :]
        else:
            top = upper[at - 3 * BLOCK : at - 3 * BLOCK + SUB, :]
        buffer[at : at + SUB, :] = top / (run + state)
        state = ends[s : s + 1, :] * (state + run[SUB - 1 : SUB, :])
        if (at + SUB) % rows == 0:
            c = at // rows
            part = pl.ds(c * rows, rows)
            copy = pltpu.make_async_copy(buffer.at[part, :], out.at[part, :], sems.at[c])
            copy.start()
            copies.append(copy)
    for copy in copies:
        copy.wait()


def body(raw, band_taps, real_taps, imag_taps, short_taps, lta_rate, lta_start, gap_gain):
    f32, bf16 = jnp.float32, jnp.bfloat16
    struct = jax.ShapeDtypeStruct
    signal = lax.all_to_all(raw, "chan", split_axis=1, concat_axis=0, tiled=True)
    total, cols = signal.shape
    count, subs = total // BLOCK, total // SUB
    groups = lax.axis_size("tm")

    taps = jnp.stack([band_taps, real_taps, imag_taps, short_taps]).astype(f32)
    tap_rows = jnp.pad(taps[:, ::-1], ((0, 0), (1, BLOCK - 1)))
    band_m, pair_m, short_m, sums_m = call(
        matrices_kernel,
        [
            struct((BLOCK, 2 * BLOCK), bf16),
            struct((2 * BLOCK, 2 * BLOCK), bf16),
            struct((BLOCK, 2 * BLOCK), bf16),
            struct((BLOCK, 2 * BLOCK), bf16),
        ],
        [VMEM],
    )(tap_rows)

    keep_log = jnp.log1p(-(1.0 - (1.0 - lta_rate)))
    offsets = (jnp.arange(BLOCK) % SUB + 1).astype(f32)
    scale = jnp.exp(-offsets[:, None] * keep_log[None, :])
    rate_scale = scale * lta_rate[None, :]
    gain = jnp.cumprod(gap_gain.reshape(subs, SUB), axis=1)
    gain_scale = jnp.broadcast_to((1.0 / gain).reshape(total, 1), (total, 128))
    ends = jnp.exp(SUB * keep_log)[None, :] * gain[:, SUB - 1 :]

    prior = from_behind(signal[total - 2 * BLOCK :], "tm")
    band1, energy2, energy_last, running, upper = call(
        functools.partial(main_kernel, count),
        [
            struct((BLOCK, cols), bf16),
            struct((BLOCK, cols), bf16),
            struct((BLOCK, cols), bf16),
            struct((total - 2 * BLOCK, cols), f32),
            struct((total - 3 * BLOCK, cols), f32),
        ],
        [VMEM] * 8,
        scratch=[pltpu.VMEM((total, cols), bf16), pltpu.VMEM((total, cols), bf16)],
    )(signal, band_m, pair_m, short_m, sums_m, rate_scale, scale, gain_scale)
    energy_before = from_behind(energy_last, "tm")
    energy0, running01, upper12, totals = call(
        functools.partial(edge_kernel, subs),
        [
            struct((BLOCK, cols), bf16),
            struct((2 * BLOCK, cols), f32),
            struct((2 * BLOCK, cols), f32),
            struct((groups, 2, cols), f32),
        ],
        [VMEM] * 13,
    )(prior, signal, band1, energy2, running, band_m, pair_m, short_m, sums_m,
      rate_scale, scale, gain_scale, ends)
    totals = lax.all_to_all(totals, "tm", split_axis=0, concat_axis=0, tiled=True)
    position = lax.axis_index("tm").astype(jnp.int32).reshape(1)
    chunks = 4
    return call(
        functools.partial(ratio_kernel, subs, chunks),
        struct((total, cols), f32),
        [SMEM] + [VMEM] * 12,
        out_specs=pl.BlockSpec(memory_space=pl.ANY),
        scratch=[pltpu.VMEM((total, cols), f32), pltpu.SemaphoreType.DMA((chunks,))],
    )(position, totals, lta_start.reshape(1, cols), energy_before, energy0, running01, running,
      upper12, upper, short_m, scale, gain_scale, ends)


def solution(mesh):
    return jax.shard_map(
        body,
        mesh=mesh,
        in_specs=(P(("tm", "chan"), None), P(), P(), P(), P(), P("chan"), P("chan"), P("tm")),
        out_specs=P("tm", "chan"),
        check_vma=False,
    )
```

```python
import functools

import jax
import jax.numpy as jnp
from jax import lax
from jax.experimental import pallas as pl
from jax.experimental.pallas import tpu as pltpu
from jax.sharding import PartitionSpec as P

BLOCK = 128
SUB = 64
VMEM = pl.BlockSpec(memory_space=pltpu.VMEM)
SMEM = pl.BlockSpec(memory_space=pltpu.SMEM)
ANY = pl.BlockSpec(memory_space=pl.ANY)
HBM = pl.BlockSpec(memory_space=pltpu.HBM)


def dot(a, b):
    return jnp.dot(a, b, preferred_element_type=jnp.float32)


def call(kernel, out_shape, in_specs, out_specs=None, scratch=(), limit=24):
    if out_specs is None:
        out_specs = jax.tree.map(lambda _: VMEM, out_shape)
    return pl.pallas_call(
        kernel,
        out_shape=out_shape,
        in_specs=in_specs,
        out_specs=out_specs,
        scratch_shapes=scratch,
        compiler_params=pltpu.CompilerParams(vmem_limit_bytes=limit * 1024 * 1024),
    )


def from_behind(value, axis):
    count = lax.axis_size(axis)
    return lax.ppermute(value, axis, [(source, source + 1) for source in range(count - 1)])


def regroup_kernel(raw, out, held, sems):
    groups, _, cols = out.shape
    count = sems.shape[0]
    each = groups // count
    copies = []
    for c in range(count):
        part = pl.ds(c * each * cols, each * cols)
        copies.append(pltpu.make_async_copy(raw.at[:, part], held.at[:, part], sems.at[c]))
    for copy in copies:
        copy.start()
    for c, copy in enumerate(copies):
        copy.wait()
        for k in range(c * each, (c + 1) * each):
            out[k] = held[:, k * cols : (k + 1) * cols]


def prepare_kernel(
    band_taps, real_taps, imag_taps, short_taps, keep_log, gap_gain,
    band_ref, pair_ref, short_ref, sums_ref, scale, gain_scale, ends,
):
    def toeplitz(taps):
        row = jnp.concatenate([taps[...].astype(jnp.float32), jnp.zeros((1, BLOCK))], axis=1)
        rows = pltpu.roll(
            jnp.broadcast_to(row, (2 * BLOCK, 2 * BLOCK)), BLOCK, 1, stride=1, stride_axis=0
        )
        return rows[:, :BLOCK].T.astype(jnp.bfloat16)

    band_ref[...] = toeplitz(band_taps)
    pair_ref[:BLOCK, :] = toeplitz(real_taps)
    pair_ref[BLOCK:, :] = toeplitz(imag_taps)
    short_ref[...] = toeplitz(short_taps)
    row = lax.broadcasted_iota(jnp.int32, (BLOCK, 2 * BLOCK), 0)
    col = lax.broadcasted_iota(jnp.int32, (BLOCK, 2 * BLOCK), 1) % BLOCK
    keep = (col <= row) & (col // SUB == row // SUB)
    sums_ref[...] = jnp.where(keep, 1.0, 0.0).astype(jnp.bfloat16)
    offset = (lax.broadcasted_iota(jnp.int32, scale.shape, 0) + 1).astype(jnp.float32)
    scale[...] = jnp.exp(-offset * keep_log[...])
    gain = gap_gain[...]
    place = lax.broadcasted_iota(jnp.int32, gain.shape, 1) % SUB
    reach = 1
    while reach < SUB:
        gain = gain * jnp.where(place >= reach, pltpu.roll(gain, reach, 1), 1.0)
        reach *= 2
    inverse = 1.0 / gain
    whole = jnp.exp(SUB * keep_log[...])
    for b in range(gain.shape[0]):
        column = jnp.broadcast_to(inverse[b : b + 1, :], (BLOCK, BLOCK)).T
        gain_scale[block(b), :] = column
        for h in range(BLOCK // SUB):
            s = b * (BLOCK // SUB) + h
            last = column[(h + 1) * SUB - 1 : (h + 1) * SUB, :]
            lanes = jnp.concatenate([1.0 / last] * (ends.shape[1] // BLOCK), axis=1)
            ends[s : s + 1, :] = whole * lanes


def energy_of(pair, window):
    both = dot(pair, window)
    real, imag = both[:BLOCK], both[BLOCK:]
    return (real * real + imag * imag).astype(jnp.bfloat16)


def inverse_decay(scale, gain_scale):
    cols = scale.shape[1]
    lanes = jnp.concatenate([gain_scale] * (cols // 128), axis=1)
    return jnp.concatenate([scale] * (BLOCK // SUB), axis=0) * lanes


def scaled_energy(energy, rate, scale, gain_scale):
    return energy.astype(jnp.float32) * (inverse_decay(scale, gain_scale) * rate)


def last_sums(scaled):
    return [
        jnp.sum(scaled[h * SUB : (h + 1) * SUB, :], axis=0, keepdims=True)
        for h in range(BLOCK // SUB)
    ]


def block(b, n=1):
    return pl.ds(b * BLOCK, n * BLOCK)


def main_kernel(
    count, signal, band_m, pair_m, rate, scale, gain_scale, band1, energy, energy_last, tails, band
):
    for b in range(1, count):
        band[block(b), :] = dot(band_m[...], signal[block(b - 1, 2), :]).astype(jnp.bfloat16)
    band1[...] = band[block(1), :]
    for b in range(2, count):
        e = energy_of(pair_m[...], band[block(b - 1, 2), :])
        energy[block(b - 2), :] = e
        if b == count - 1:
            energy_last[...] = e
        sums = last_sums(scaled_energy(e, rate[...], scale[...], gain_scale[block(b), :]))
        for h, row in enumerate(sums):
            at = (b - 2) * len(sums) + h
            tails[at : at + 1, :] = row


def edge_kernel(
    subs, prior_any, signal, band1, tails, band_m, pair_m, rate, scale, gain_scale, ends,
    energy, totals, window, sem,
):
    copy = pltpu.make_async_copy(prior_any, window.at[block(0, 2), :], sem)
    copy.start()
    window[block(2), :] = signal[block(0), :]
    copy.wait()
    band = [
        dot(band_m[...], window[block(b, 2), :]).astype(jnp.bfloat16) for b in range(2)
    ] + [band1[...]]
    rows = []
    for b in range(2):
        e = energy_of(pair_m[...], jnp.concatenate([band[b], band[b + 1]], axis=0))
        energy[block(b), :] = e
        rows += last_sums(scaled_energy(e, rate[...], scale[...], gain_scale[block(b), :]))
    edge = len(rows)
    value = jnp.zeros_like(ends[0:1, :])
    decay = jnp.ones_like(value)
    for s in range(subs):
        end = rows[s] if s < edge else tails[s - edge : s - edge + 1, :]
        step = ends[s : s + 1, :]
        value = step * (value + end)
        decay = decay * step
    both = jnp.concatenate([decay, value], axis=0)
    for k in range(totals.shape[0]):
        totals[k] = both


def ratio_kernel(
    count, position, totals, start, before, head, rest, short_m, sums_m, rate, scale, gain_scale,
    ends, out, buffer, sems,
):
    parts = sems.shape[0]
    each = count // parts
    state = start[...]
    for k in range(totals.shape[0]):
        new = totals[k, 0:1, :] * state + totals[k, 1:2, :]
        state = jnp.where(k < position[0], new, state)

    def energy(b):
        return before[...] if b < 0 else head[block(b), :] if b < 2 else rest[block(b - 2), :]

    sends = []
    for b in range(count):
        current = energy(b)
        inverse = inverse_decay(scale[...], gain_scale[block(b), :])
        scaled = current.astype(jnp.float32) * (inverse * rate[...])
        high = scaled.astype(jnp.bfloat16)
        low = (scaled - high.astype(jnp.float32)).astype(jnp.bfloat16)
        running = dot(sums_m[...], jnp.concatenate([high, low], axis=0))
        window = rest[block(b - 3, 2), :] if b > 2 else jnp.concatenate([energy(b - 1), current], axis=0)
        upper = dot(short_m[...], window) * inverse
        for h in range(BLOCK // SUB):
            at = b * BLOCK + h * SUB
            run = running[h * SUB : (h + 1) * SUB, :]
            buffer[at : at + SUB, :] = upper[h * SUB : (h + 1) * SUB, :] / (run + state)
            s = at // SUB
            state = ends[s : s + 1, :] * (state + run[SUB - 1 : SUB, :])
        if (b + 1) % each == 0:
            c = b // each
            part = block(c * each, each)
            copy = pltpu.make_async_copy(buffer.at[part, :], out.at[part, :], sems.at[c])
            copy.start()
            sends.append(copy)
    for copy in sends:
        copy.wait()


def body(raw, band_taps, real_taps, imag_taps, short_taps, lta_rate, lta_start, gap_gain):
    f32, bf16 = jnp.float32, jnp.bfloat16
    struct = jax.ShapeDtypeStruct
    hbm = lambda x: pltpu.with_memory_space_constraint(x, pltpu.HBM)
    parts, groups = lax.axis_size("chan"), lax.axis_size("tm")
    held, cols = raw.shape[0], raw.shape[1] // parts
    total = held * parts
    count, subs = total // BLOCK, total // SUB
    grouped = call(
        regroup_kernel,
        pltpu.VMEM((parts, held, cols), bf16),
        [HBM],
        out_specs=VMEM,
        scratch=[pltpu.VMEM(raw.shape, bf16), pltpu.SemaphoreType.DMA((min(16, parts),))],
    )(hbm(raw))
    signal = lax.all_to_all(grouped, "chan", split_axis=0, concat_axis=0, tiled=True)
    signal = signal.reshape(total, cols)

    given = (band_taps, real_taps, imag_taps, short_taps, lta_rate, gap_gain)
    signal, given = lax.optimization_barrier((signal, given))
    band_taps, real_taps, imag_taps, short_taps, lta_rate, gap_gain = given
    taps = [x.reshape(1, BLOCK) for x in (band_taps, real_taps, imag_taps, short_taps)]
    keep_log = jnp.log1p(-(1.0 - (1.0 - lta_rate))).reshape(1, cols)
    rate = lta_rate.reshape(1, cols)
    matrix = struct((BLOCK, 2 * BLOCK), bf16)
    band_m, pair_m, short_m, sums_m, scale, gain_scale, ends = call(
        prepare_kernel,
        [
            matrix,
            struct((2 * BLOCK, 2 * BLOCK), bf16),
            matrix,
            matrix,
            struct((SUB, cols), f32),
            struct((total, 128), f32),
            struct((subs, cols), f32),
        ],
        [VMEM] * 6,
    )(*taps, keep_log, gap_gain.reshape(count, BLOCK))

    prior = from_behind(signal[total - 2 * BLOCK :], "tm")
    band1, rest, energy_last, tails = call(
        functools.partial(main_kernel, count),
        [
            struct((BLOCK, cols), bf16),
            struct((total - 2 * BLOCK, cols), bf16),
            struct((BLOCK, cols), bf16),
            struct((subs - 2 * BLOCK // SUB, cols), f32),
        ],
        [VMEM] * 6,
        scratch=[pltpu.VMEM((total, cols), bf16)],
    )(signal, band_m, pair_m, rate, scale, gain_scale)
    energy_before = from_behind(energy_last, "tm")
    head, totals = call(
        functools.partial(edge_kernel, subs),
        [struct((2 * BLOCK, cols), bf16), pltpu.VMEM((groups, 2, cols), f32)],
        [ANY] + [VMEM] * 9,
        scratch=[pltpu.VMEM((3 * BLOCK, cols), bf16), pltpu.SemaphoreType.DMA],
    )(prior, signal, band1, tails, band_m, pair_m, rate, scale, gain_scale, ends)
    totals = lax.all_to_all(totals, "tm", split_axis=0, concat_axis=0, tiled=True)
    position = lax.axis_index("tm").astype(jnp.int32).reshape(1)
    return call(
        functools.partial(ratio_kernel, count),
        pltpu.HBM((total, cols), f32),
        [SMEM] + [VMEM] * 11,
        out_specs=HBM,
        scratch=[pltpu.VMEM((total, cols), f32), pltpu.SemaphoreType.DMA((4,))],
    )(position, totals, lta_start.reshape(1, cols), energy_before, head, rest, short_m, sums_m, rate,
      scale, gain_scale, ends)


def solution(mesh):
    return jax.shard_map(
        body,
        mesh=mesh,
        in_specs=(P(("tm", "chan"), None), P(), P(), P(), P(), P("chan"), P("chan"), P("tm")),
        out_specs=P("tm", "chan"),
        check_vma=False,
    )
```

```python
import functools

import jax
import jax.numpy as jnp
from jax import lax
from jax.experimental import pallas as pl
from jax.experimental.pallas import tpu as pltpu
from jax.sharding import PartitionSpec as P

BLOCK = 128
SUB = 64
VMEM = pl.BlockSpec(memory_space=pltpu.VMEM)
SMEM = pl.BlockSpec(memory_space=pltpu.SMEM)
ANY = pl.BlockSpec(memory_space=pl.ANY)
HBM = pl.BlockSpec(memory_space=pltpu.HBM)


def dot(a, b):
    return jnp.dot(a, b, preferred_element_type=jnp.float32)


def call(kernel, out_shape, in_specs, out_specs=None, scratch=(), limit=24):
    if out_specs is None:
        out_specs = jax.tree.map(lambda _: VMEM, out_shape)
    return pl.pallas_call(
        kernel,
        out_shape=out_shape,
        in_specs=in_specs,
        out_specs=out_specs,
        scratch_shapes=scratch,
        compiler_params=pltpu.CompilerParams(vmem_limit_bytes=limit * 1024 * 1024),
    )


def from_behind(value, axis):
    count = lax.axis_size(axis)
    return lax.ppermute(value, axis, [(source, source + 1) for source in range(count - 1)])


def regroup_kernel(raw, out, held, sems):
    groups, rows, cols = out.shape
    count = sems.shape[0]
    each = rows // count
    copies = []
    for c in range(count):
        part = pl.ds(c * each, each)
        copies.append(pltpu.make_async_copy(raw.at[part, :], held.at[part, :], sems.at[c]))
    for copy in copies:
        copy.start()
    for c, copy in enumerate(copies):
        copy.wait()
        part = pl.ds(c * each, each)
        for k in range(groups):
            out[k, part, :] = held[part, k * cols : (k + 1) * cols]


def prepare_kernel(
    band_taps, real_taps, imag_taps, short_taps, keep_log, gap_gain,
    band_ref, pair_ref, short_ref, sums_ref, scale, gain_scale, ends,
):
    def toeplitz(taps):
        row = jnp.concatenate([taps[...].astype(jnp.float32), jnp.zeros((1, BLOCK))], axis=1)
        rows = pltpu.roll(
            jnp.broadcast_to(row, (2 * BLOCK, 2 * BLOCK)), BLOCK, 1, stride=1, stride_axis=0
        )
        return rows[:, :BLOCK].T.astype(jnp.bfloat16)

    band_ref[...] = toeplitz(band_taps)
    pair_ref[:BLOCK, :] = toeplitz(real_taps)
    pair_ref[BLOCK:, :] = toeplitz(imag_taps)
    short_ref[...] = toeplitz(short_taps)
    row = lax.broadcasted_iota(jnp.int32, (BLOCK, 2 * BLOCK), 0)
    col = lax.broadcasted_iota(jnp.int32, (BLOCK, 2 * BLOCK), 1) % BLOCK
    keep = (col <= row) & (col // SUB == row // SUB)
    sums_ref[...] = jnp.where(keep, 1.0, 0.0).astype(jnp.bfloat16)
    offset = (lax.broadcasted_iota(jnp.int32, scale.shape, 0) + 1).astype(jnp.float32)
    scale[...] = jnp.exp(-offset * keep_log[...])
    gain = gap_gain[...]
    place = lax.broadcasted_iota(jnp.int32, gain.shape, 1) % SUB
    reach = 1
    while reach < SUB:
        gain = gain * jnp.where(place >= reach, pltpu.roll(gain, reach, 1), 1.0)
        reach *= 2
    inverse = 1.0 / gain
    whole = jnp.exp(SUB * keep_log[...])
    for b in range(gain.shape[0]):
        column = jnp.broadcast_to(inverse[b : b + 1, :], (BLOCK, BLOCK)).T
        gain_scale[block(b), :] = column
        for h in range(BLOCK // SUB):
            s = b * (BLOCK // SUB) + h
            last = column[(h + 1) * SUB - 1 : (h + 1) * SUB, :]
            lanes = jnp.concatenate([1.0 / last] * (ends.shape[1] // BLOCK), axis=1)
            ends[s : s + 1, :] = whole * lanes


def halo_kernel(signal, halo):
    halo[...] = signal[signal.shape[0] - halo.shape[0] :, :]


def energy_of(pair, window):
    both = dot(pair, window)
    real, imag = both[:BLOCK], both[BLOCK:]
    return (real * real + imag * imag).astype(jnp.bfloat16)


def inverse_decay(scale, gain_scale):
    cols = scale.shape[1]
    lanes = jnp.concatenate([gain_scale] * (cols // 128), axis=1)
    return jnp.concatenate([scale] * (BLOCK // SUB), axis=0) * lanes


def scaled_energy(energy, rate, scale, gain_scale):
    return energy.astype(jnp.float32) * (inverse_decay(scale, gain_scale) * rate)


def last_sums(scaled):
    return [
        jnp.sum(scaled[h * SUB : (h + 1) * SUB, :], axis=0, keepdims=True)
        for h in range(BLOCK // SUB)
    ]


def block(b, n=1):
    return pl.ds(b * BLOCK, n * BLOCK)


def main_kernel(
    count, signal, band_m, pair_m, rate, scale, gain_scale, band1, energy, energy_last, tails, band,
    energy_v, tails_v, sems,
):
    for b in range(1, count):
        band[block(b), :] = dot(band_m[...], signal[block(b - 1, 2), :]).astype(jnp.bfloat16)
    band1[...] = band[block(1), :]
    order = [count - 1, *range(2, count - 1)]
    half = len(order) // 2
    copies = []

    def send(source, target):
        copy = pltpu.make_async_copy(source, target, sems.at[len(copies)])
        copy.start()
        copies.append(copy)

    for done, b in enumerate(order):
        e = energy_of(pair_m[...], band[block(b - 1, 2), :])
        energy_v[block(b - 2), :] = e
        sums = last_sums(scaled_energy(e, rate[...], scale[...], gain_scale[block(b), :]))
        for h, row in enumerate(sums):
            at = (b - 2) * len(sums) + h
            tails_v[at : at + 1, :] = row
        if done == 0:
            send(energy_v.at[block(count - 3), :], energy_last)
        if done == half:
            send(energy_v.at[block(0, half), :], energy.at[block(0, half), :])
    send(tails_v, tails)
    part = block(half, count - 2 - half)
    send(energy_v.at[part, :], energy.at[part, :])
    for copy in copies:
        copy.wait()


def edge_kernel(
    subs, prior_any, signal, band1, tails_hbm, band_m, pair_m, rate, scale, gain_scale, ends,
    energy, totals, window, tails, sems,
):
    copy = pltpu.make_async_copy(prior_any, window.at[block(0, 2), :], sems.at[0])
    copy.start()
    fetch = pltpu.make_async_copy(tails_hbm, tails, sems.at[1])
    fetch.start()
    window[block(2), :] = signal[block(0), :]
    copy.wait()
    band = [
        dot(band_m[...], window[block(b, 2), :]).astype(jnp.bfloat16) for b in range(2)
    ] + [band1[...]]
    rows = []
    for b in range(2):
        e = energy_of(pair_m[...], jnp.concatenate([band[b], band[b + 1]], axis=0))
        energy[block(b), :] = e
        rows += last_sums(scaled_energy(e, rate[...], scale[...], gain_scale[block(b), :]))
    edge = len(rows)
    fetch.wait()
    value = jnp.zeros_like(ends[0:1, :])
    decay = jnp.ones_like(value)
    for s in range(subs):
        end = rows[s] if s < edge else tails[s - edge : s - edge + 1, :]
        step = ends[s : s + 1, :]
        value = step * (value + end)
        decay = decay * step
    both = jnp.concatenate([decay, value], axis=0)
    for k in range(totals.shape[0]):
        totals[k] = both


def carry_kernel(position, totals, start, carry):
    state = start[...]
    for k in range(totals.shape[0]):
        new = totals[k, 0:1, :] * state + totals[k, 1:2, :]
        state = jnp.where(k < position[0], new, state)
    carry[...] = state


def ratio_kernel(
    count, carry, before, head, rest, short_m, sums_m, rate, scale, gain_scale,
    ends, out, buffer, sems,
):
    parts = sems.shape[0]
    each = count // parts
    state = carry[...]

    def energy(b):
        return before[...] if b < 0 else head[block(b), :] if b < 2 else rest[block(b - 2), :]

    sends = []
    for b in range(count):
        current = energy(b)
        inverse = inverse_decay(scale[...], gain_scale[block(b), :])
        scaled = current.astype(jnp.float32) * (inverse * rate[...])
        high = scaled.astype(jnp.bfloat16)
        low = (scaled - high.astype(jnp.float32)).astype(jnp.bfloat16)
        running = dot(sums_m[...], jnp.concatenate([high, low], axis=0))
        window = rest[block(b - 3, 2), :] if b > 2 else jnp.concatenate([energy(b - 1), current], axis=0)
        upper = dot(short_m[...], window) * inverse
        for h in range(BLOCK // SUB):
            at = b * BLOCK + h * SUB
            run = running[h * SUB : (h + 1) * SUB, :]
            buffer[at : at + SUB, :] = upper[h * SUB : (h + 1) * SUB, :] / (run + state)
            s = at // SUB
            state = ends[s : s + 1, :] * (state + run[SUB - 1 : SUB, :])
        if (b + 1) % each == 0:
            c = b // each
            part = block(c * each, each)
            copy = pltpu.make_async_copy(buffer.at[part, :], out.at[part, :], sems.at[c])
            copy.start()
            sends.append(copy)
    for copy in sends:
        copy.wait()


def body(raw, band_taps, real_taps, imag_taps, short_taps, lta_rate, lta_start, gap_gain):
    f32, bf16 = jnp.float32, jnp.bfloat16
    struct = jax.ShapeDtypeStruct
    hbm = lambda x: pltpu.with_memory_space_constraint(x, pltpu.HBM)
    parts, groups = lax.axis_size("chan"), lax.axis_size("tm")
    held, cols = raw.shape[0], raw.shape[1] // parts
    total = held * parts
    count, subs = total // BLOCK, total // SUB
    grouped = call(
        regroup_kernel,
        pltpu.VMEM((parts, held, cols), bf16),
        [HBM],
        out_specs=VMEM,
        scratch=[pltpu.VMEM(raw.shape, bf16), pltpu.SemaphoreType.DMA((3,))],
    )(hbm(raw))
    signal = lax.all_to_all(grouped, "chan", split_axis=0, concat_axis=0, tiled=True)
    signal = signal.reshape(total, cols)

    given = (band_taps, real_taps, imag_taps, short_taps, lta_rate, gap_gain)
    signal, given = lax.optimization_barrier((signal, given))
    band_taps, real_taps, imag_taps, short_taps, lta_rate, gap_gain = given
    taps = [x.reshape(1, BLOCK) for x in (band_taps, real_taps, imag_taps, short_taps)]
    keep_log = jnp.log1p(-(1.0 - (1.0 - lta_rate))).reshape(1, cols)
    rate = lta_rate.reshape(1, cols)
    matrix = struct((BLOCK, 2 * BLOCK), bf16)
    band_m, pair_m, short_m, sums_m, scale, gain_scale, ends = call(
        prepare_kernel,
        [
            matrix,
            struct((2 * BLOCK, 2 * BLOCK), bf16),
            matrix,
            matrix,
            struct((SUB, cols), f32),
            struct((total, 128), f32),
            struct((subs, cols), f32),
        ],
        [VMEM] * 6,
    )(*taps, keep_log, gap_gain.reshape(count, BLOCK))

    halo = call(halo_kernel, pltpu.VMEM((2 * BLOCK, cols), bf16), [VMEM])(signal)
    prior = from_behind(halo, "tm")
    band1, rest, energy_last, tails = call(
        functools.partial(main_kernel, count),
        [
            struct((BLOCK, cols), bf16),
            pltpu.HBM((total - 2 * BLOCK, cols), bf16),
            pltpu.HBM((BLOCK, cols), bf16),
            pltpu.HBM((subs - 2 * BLOCK // SUB, cols), f32),
        ],
        [VMEM] * 6,
        out_specs=[VMEM, HBM, HBM, HBM],
        scratch=[
            pltpu.VMEM((total, cols), bf16),
            pltpu.VMEM((total - 2 * BLOCK, cols), bf16),
            pltpu.VMEM((subs - 2 * BLOCK // SUB, cols), f32),
            pltpu.SemaphoreType.DMA((4,)),
        ],
    )(signal, band_m, pair_m, rate, scale, gain_scale)
    energy_before = from_behind(energy_last, "tm")
    head, totals = call(
        functools.partial(edge_kernel, subs),
        [struct((2 * BLOCK, cols), bf16), pltpu.VMEM((groups, 2, cols), f32)],
        [ANY] + [VMEM] * 2 + [HBM] + [VMEM] * 6,
        scratch=[
            pltpu.VMEM((3 * BLOCK, cols), bf16),
            pltpu.VMEM((subs - 2 * BLOCK // SUB, cols), f32),
            pltpu.SemaphoreType.DMA((2,)),
        ],
    )(prior, signal, band1, hbm(tails), band_m, pair_m, rate, scale, gain_scale, ends)
    position = lax.axis_index("tm").astype(jnp.int32).reshape(1)
    totals, position, start = lax.optimization_barrier(
        (totals, position, lta_start.reshape(1, cols))
    )
    totals = lax.all_to_all(totals, "tm", split_axis=0, concat_axis=0, tiled=True)
    carry = call(
        carry_kernel, struct((1, cols), f32), [SMEM] + [VMEM] * 2
    )(position, totals, start)
    return call(
        functools.partial(ratio_kernel, count),
        pltpu.HBM((total, cols), f32),
        [VMEM] * 10,
        out_specs=HBM,
        scratch=[pltpu.VMEM((total, cols), f32), pltpu.SemaphoreType.DMA((12,))],
    )(carry, energy_before, head, rest, short_m, sums_m, rate,
      scale, gain_scale, ends)


def solution(mesh):
    return jax.shard_map(
        body,
        mesh=mesh,
        in_specs=(P(("tm", "chan"), None), P(), P(), P(), P(), P("chan"), P("chan"), P("tm")),
        out_specs=P("tm", "chan"),
        check_vma=False,
    )
```

```python
import functools

import jax
import jax.numpy as jnp
from jax import lax
from jax.experimental import pallas as pl
from jax.experimental.pallas import tpu as pltpu
from jax.sharding import PartitionSpec as P

BLOCK = 128
SUB = 64
VMEM = pl.BlockSpec(memory_space=pltpu.VMEM)
SMEM = pl.BlockSpec(memory_space=pltpu.SMEM)
ANY = pl.BlockSpec(memory_space=pl.ANY)
HBM = pl.BlockSpec(memory_space=pltpu.HBM)


def dot(a, b):
    return jnp.dot(a, b, preferred_element_type=jnp.float32)


def call(kernel, out_shape, in_specs, out_specs=None, scratch=(), limit=24):
    if out_specs is None:
        out_specs = jax.tree.map(lambda _: VMEM, out_shape)
    return pl.pallas_call(
        kernel,
        out_shape=out_shape,
        in_specs=in_specs,
        out_specs=out_specs,
        scratch_shapes=scratch,
        compiler_params=pltpu.CompilerParams(vmem_limit_bytes=limit * 1024 * 1024),
    )


def from_behind(value, axis):
    count = lax.axis_size(axis)
    return lax.ppermute(value, axis, [(source, source + 1) for source in range(count - 1)])


def regroup_kernel(raw, out, held, sems):
    groups, rows, cols = out.shape
    count = sems.shape[0]
    each = rows // count
    copies = []
    for c in range(count):
        part = pl.ds(c * each, each)
        copies.append(pltpu.make_async_copy(raw.at[part, :], held.at[part, :], sems.at[c]))
    for copy in copies:
        copy.start()
    for c, copy in enumerate(copies):
        copy.wait()
        part = pl.ds(c * each, each)
        for k in range(groups):
            out[k, part, :] = held[part, k * cols : (k + 1) * cols]


def prepare_kernel(
    band_taps, real_taps, imag_taps, short_taps, keep_log, gap_gain,
    band_ref, pair_ref, short_ref, sums_ref, scale, gain_scale, ends,
):
    def toeplitz(taps):
        row = jnp.concatenate([taps[...].astype(jnp.float32), jnp.zeros((1, BLOCK))], axis=1)
        rows = pltpu.roll(
            jnp.broadcast_to(row, (2 * BLOCK, 2 * BLOCK)), BLOCK, 1, stride=1, stride_axis=0
        )
        return rows[:, :BLOCK].T.astype(jnp.bfloat16)

    band_ref[...] = toeplitz(band_taps)
    pair_ref[:BLOCK, :] = toeplitz(real_taps)
    pair_ref[BLOCK:, :] = toeplitz(imag_taps)
    short_ref[...] = toeplitz(short_taps)
    row = lax.broadcasted_iota(jnp.int32, (BLOCK, 2 * BLOCK), 0)
    col = lax.broadcasted_iota(jnp.int32, (BLOCK, 2 * BLOCK), 1) % BLOCK
    keep = (col <= row) & (col // SUB == row // SUB)
    sums_ref[...] = jnp.where(keep, 1.0, 0.0).astype(jnp.bfloat16)
    offset = (lax.broadcasted_iota(jnp.int32, scale.shape, 0) + 1).astype(jnp.float32)
    scale[...] = jnp.exp(-offset * keep_log[...])
    gain = gap_gain[...]
    place = lax.broadcasted_iota(jnp.int32, gain.shape, 1) % SUB
    reach = 1
    while reach < SUB:
        gain = gain * jnp.where(place >= reach, pltpu.roll(gain, reach, 1), 1.0)
        reach *= 2
    inverse = 1.0 / gain
    whole = jnp.exp(SUB * keep_log[...])
    for b in range(gain.shape[0]):
        column = jnp.broadcast_to(inverse[b : b + 1, :], (BLOCK, BLOCK)).T
        gain_scale[block(b), :] = column
        for h in range(BLOCK // SUB):
            s = b * (BLOCK // SUB) + h
            last = column[(h + 1) * SUB - 1 : (h + 1) * SUB, :]
            lanes = jnp.concatenate([1.0 / last] * (ends.shape[1] // BLOCK), axis=1)
            ends[s : s + 1, :] = whole * lanes


def halo_kernel(signal, halo):
    halo[...] = signal[signal.shape[0] - halo.shape[0] :, :]


def energy_of(pair, window):
    both = dot(pair, window)
    real, imag = both[:BLOCK], both[BLOCK:]
    return (real * real + imag * imag).astype(jnp.bfloat16)


def inverse_decay(scale, gain_scale):
    cols = scale.shape[1]
    lanes = jnp.concatenate([gain_scale] * (cols // 128), axis=1)
    return jnp.concatenate([scale] * (BLOCK // SUB), axis=0) * lanes


def scaled_energy(energy, rate, scale, gain_scale):
    return energy.astype(jnp.float32) * (inverse_decay(scale, gain_scale) * rate)


def last_sums(scaled):
    return [
        jnp.sum(scaled[h * SUB : (h + 1) * SUB, :], axis=0, keepdims=True)
        for h in range(BLOCK // SUB)
    ]


def block(b, n=1):
    return pl.ds(b * BLOCK, n * BLOCK)


def compose(sums, ends):
    value = jnp.zeros_like(ends[0:1, :])
    decay = jnp.ones_like(value)
    for s, row in sums:
        step = ends[s : s + 1, :]
        value = step * (value + row)
        decay = decay * step
    return jnp.concatenate([decay, value], axis=0)


def main_kernel(
    count, signal, band_m, pair_m, rate, scale, gain_scale, ends, band1, energy, energy_last, tail, band,
    energy_v, sems,
):
    for b in range(1, count):
        band[block(b), :] = dot(band_m[...], signal[block(b - 1, 2), :]).astype(jnp.bfloat16)
    band1[...] = band[block(1), :]
    order = [count - 1, *range(2, count - 1)]
    half = len(order) // 2
    copies = []
    tails = {}

    def send(source, target):
        copy = pltpu.make_async_copy(source, target, sems.at[len(copies)])
        copy.start()
        copies.append(copy)

    for done, b in enumerate(order):
        e = energy_of(pair_m[...], band[block(b - 1, 2), :])
        energy_v[block(b - 2), :] = e
        sums = last_sums(scaled_energy(e, rate[...], scale[...], gain_scale[block(b), :]))
        for h, row in enumerate(sums):
            tails[b * len(sums) + h] = row
        if done == 0:
            send(energy_v.at[block(count - 3), :], energy_last)
        if done == half:
            send(energy_v.at[block(0, half), :], energy.at[block(0, half), :])
    part = block(half, count - 2 - half)
    send(energy_v.at[part, :], energy.at[part, :])
    tail[...] = compose(sorted(tails.items()), ends)
    for copy in copies:
        copy.wait()


def edge_kernel(
    prior_any, signal, band1, tail, band_m, pair_m, rate, scale, gain_scale, ends,
    energy, totals, window, sem,
):
    copy = pltpu.make_async_copy(prior_any, window.at[block(0, 2), :], sem)
    copy.start()
    window[block(2), :] = signal[block(0), :]
    copy.wait()
    band = [
        dot(band_m[...], window[block(b, 2), :]).astype(jnp.bfloat16) for b in range(2)
    ] + [band1[...]]
    rows = []
    for b in range(2):
        e = energy_of(pair_m[...], jnp.concatenate([band[b], band[b + 1]], axis=0))
        energy[block(b), :] = e
        rows += last_sums(scaled_energy(e, rate[...], scale[...], gain_scale[block(b), :]))
    first = compose(list(enumerate(rows)), ends)
    decay, value = tail[0:1, :], tail[1:2, :]
    both = jnp.concatenate([decay * first[0:1, :], decay * first[1:2, :] + value], axis=0)
    for k in range(totals.shape[0]):
        totals[k] = both


def carry_kernel(position, totals, start, carry):
    state = start[...]
    for k in range(totals.shape[0]):
        new = totals[k, 0:1, :] * state + totals[k, 1:2, :]
        state = jnp.where(k < position[0], new, state)
    carry[...] = state


def ratio_kernel(
    count, carry, before, head, rest, short_m, sums_m, rate, scale, gain_scale,
    ends, out, buffer, sems,
):
    parts = sems.shape[0]
    each = count // parts
    state = carry[...]

    def energy(b):
        return before[...] if b < 0 else head[block(b), :] if b < 2 else rest[block(b - 2), :]

    sends = []
    for b in range(count):
        current = energy(b)
        inverse = inverse_decay(scale[...], gain_scale[block(b), :])
        scaled = current.astype(jnp.float32) * (inverse * rate[...])
        high = scaled.astype(jnp.bfloat16)
        low = (scaled - high.astype(jnp.float32)).astype(jnp.bfloat16)
        running = dot(sums_m[...], jnp.concatenate([high, low], axis=0))
        window = rest[block(b - 3, 2), :] if b > 2 else jnp.concatenate([energy(b - 1), current], axis=0)
        upper = dot(short_m[...], window) * inverse
        for h in range(BLOCK // SUB):
            at = b * BLOCK + h * SUB
            run = running[h * SUB : (h + 1) * SUB, :]
            buffer[at : at + SUB, :] = upper[h * SUB : (h + 1) * SUB, :] / (run + state)
            s = at // SUB
            state = ends[s : s + 1, :] * (state + run[SUB - 1 : SUB, :])
        if (b + 1) % each == 0:
            c = b // each
            part = block(c * each, each)
            copy = pltpu.make_async_copy(buffer.at[part, :], out.at[part, :], sems.at[c])
            copy.start()
            sends.append(copy)
    for copy in sends:
        copy.wait()


def body(raw, band_taps, real_taps, imag_taps, short_taps, lta_rate, lta_start, gap_gain):
    f32, bf16 = jnp.float32, jnp.bfloat16
    struct = jax.ShapeDtypeStruct
    hbm = lambda x: pltpu.with_memory_space_constraint(x, pltpu.HBM)
    parts, groups = lax.axis_size("chan"), lax.axis_size("tm")
    held, cols = raw.shape[0], raw.shape[1] // parts
    total = held * parts
    count, subs = total // BLOCK, total // SUB
    grouped = call(
        regroup_kernel,
        pltpu.VMEM((parts, held, cols), bf16),
        [HBM],
        out_specs=VMEM,
        scratch=[pltpu.VMEM(raw.shape, bf16), pltpu.SemaphoreType.DMA((3,))],
    )(hbm(raw))
    signal = lax.all_to_all(grouped, "chan", split_axis=0, concat_axis=0, tiled=True)
    signal = signal.reshape(total, cols)

    given = (band_taps, real_taps, imag_taps, short_taps, lta_rate, gap_gain)
    signal, given = lax.optimization_barrier((signal, given))
    band_taps, real_taps, imag_taps, short_taps, lta_rate, gap_gain = given
    taps = [x.reshape(1, BLOCK) for x in (band_taps, real_taps, imag_taps, short_taps)]
    keep_log = jnp.log1p(-(1.0 - (1.0 - lta_rate))).reshape(1, cols)
    rate = lta_rate.reshape(1, cols)
    matrix = struct((BLOCK, 2 * BLOCK), bf16)
    band_m, pair_m, short_m, sums_m, scale, gain_scale, ends = call(
        prepare_kernel,
        [
            matrix,
            struct((2 * BLOCK, 2 * BLOCK), bf16),
            matrix,
            matrix,
            struct((SUB, cols), f32),
            struct((total, 128), f32),
            struct((subs, cols), f32),
        ],
        [VMEM] * 6,
    )(*taps, keep_log, gap_gain.reshape(count, BLOCK))

    halo = call(halo_kernel, pltpu.VMEM((2 * BLOCK, cols), bf16), [VMEM])(signal)
    prior = from_behind(halo, "tm")
    band1, rest, energy_last, tail = call(
        functools.partial(main_kernel, count),
        [
            struct((BLOCK, cols), bf16),
            pltpu.HBM((total - 2 * BLOCK, cols), bf16),
            pltpu.HBM((BLOCK, cols), bf16),
            struct((2, cols), f32),
        ],
        [VMEM] * 7,
        out_specs=[VMEM, HBM, HBM, VMEM],
        scratch=[
            pltpu.VMEM((total, cols), bf16),
            pltpu.VMEM((total - 2 * BLOCK, cols), bf16),
            pltpu.SemaphoreType.DMA((3,)),
        ],
    )(signal, band_m, pair_m, rate, scale, gain_scale, ends)
    energy_before = from_behind(energy_last, "tm")
    head, totals = call(
        edge_kernel,
        [struct((2 * BLOCK, cols), bf16), pltpu.VMEM((groups, 2, cols), f32)],
        [ANY] + [VMEM] * 9,
        scratch=[pltpu.VMEM((3 * BLOCK, cols), bf16), pltpu.SemaphoreType.DMA],
    )(prior, signal, band1, tail, band_m, pair_m, rate, scale, gain_scale, ends)
    position = lax.axis_index("tm").astype(jnp.int32).reshape(1)
    totals, position, start = lax.optimization_barrier(
        (totals, position, lta_start.reshape(1, cols))
    )
    totals = lax.all_to_all(totals, "tm", split_axis=0, concat_axis=0, tiled=True)
    carry = call(
        carry_kernel, struct((1, cols), f32), [SMEM] + [VMEM] * 2
    )(position, totals, start)
    return call(
        functools.partial(ratio_kernel, count),
        pltpu.HBM((total, cols), f32),
        [VMEM] * 10,
        out_specs=HBM,
        scratch=[pltpu.VMEM((total, cols), f32), pltpu.SemaphoreType.DMA((12,))],
    )(carry, energy_before, head, rest, short_m, sums_m, rate,
      scale, gain_scale, ends)


def solution(mesh):
    return jax.shard_map(
        body,
        mesh=mesh,
        in_specs=(P(("tm", "chan"), None), P(), P(), P(), P(), P("chan"), P("chan"), P("tm")),
        out_specs=P("tm", "chan"),
        check_vma=False,
    )
```

```python
import functools

import jax
import jax.numpy as jnp
from jax import lax
from jax.experimental import pallas as pl
from jax.experimental.pallas import tpu as pltpu
from jax.sharding import PartitionSpec as P

BLOCK = 128
SUB = 64
VMEM = pl.BlockSpec(memory_space=pltpu.VMEM)
SMEM = pl.BlockSpec(memory_space=pltpu.SMEM)
ANY = pl.BlockSpec(memory_space=pl.ANY)
HBM = pl.BlockSpec(memory_space=pltpu.HBM)


def dot(a, b):
    return jnp.dot(a, b, preferred_element_type=jnp.float32)


def call(kernel, out_shape, in_specs, out_specs=None, scratch=(), limit=24):
    if out_specs is None:
        out_specs = jax.tree.map(lambda _: VMEM, out_shape)
    return pl.pallas_call(
        kernel,
        out_shape=out_shape,
        in_specs=in_specs,
        out_specs=out_specs,
        scratch_shapes=scratch,
        compiler_params=pltpu.CompilerParams(vmem_limit_bytes=limit * 1024 * 1024),
    )


def from_behind(value, axis):
    count = lax.axis_size(axis)
    return lax.ppermute(value, axis, [(source, source + 1) for source in range(count - 1)])


def regroup_kernel(raw, out, held, sems):
    groups, rows, cols = out.shape
    count = sems.shape[0]
    each = rows // count
    copies = []
    for c in range(count):
        part = pl.ds(c * each, each)
        copies.append(pltpu.make_async_copy(raw.at[part, :], held.at[part, :], sems.at[c]))
    for copy in copies:
        copy.start()
    for c, copy in enumerate(copies):
        copy.wait()
        part = pl.ds(c * each, each)
        for k in range(groups):
            out[k, part, :] = held[part, k * cols : (k + 1) * cols]


def prepare_kernel(
    band_taps, real_taps, imag_taps, short_taps, keep_log, gap_gain,
    band_ref, pair_ref, short_ref, sums_ref, scale, gain_scale, ends,
):
    def toeplitz(taps):
        row = jnp.concatenate([taps[...].astype(jnp.float32), jnp.zeros((1, BLOCK))], axis=1)
        rows = pltpu.roll(
            jnp.broadcast_to(row, (2 * BLOCK, 2 * BLOCK)), BLOCK, 1, stride=1, stride_axis=0
        )
        return rows[:, :BLOCK].T.astype(jnp.bfloat16)

    band_ref[...] = toeplitz(band_taps)
    pair_ref[:BLOCK, :] = toeplitz(real_taps)
    pair_ref[BLOCK:, :] = toeplitz(imag_taps)
    short_ref[...] = toeplitz(short_taps)
    row = lax.broadcasted_iota(jnp.int32, (BLOCK, 2 * BLOCK), 0)
    col = lax.broadcasted_iota(jnp.int32, (BLOCK, 2 * BLOCK), 1) % BLOCK
    keep = (col <= row) & (col // SUB == row // SUB)
    sums_ref[...] = jnp.where(keep, 1.0, 0.0).astype(jnp.bfloat16)
    offset = (lax.broadcasted_iota(jnp.int32, scale.shape, 0) + 1).astype(jnp.float32)
    scale[...] = jnp.exp(-offset * keep_log[...])
    gain = gap_gain[...]
    place = lax.broadcasted_iota(jnp.int32, gain.shape, 1) % SUB
    reach = 1
    while reach < SUB:
        gain = gain * jnp.where(place >= reach, pltpu.roll(gain, reach, 1), 1.0)
        reach *= 2
    inverse = 1.0 / gain
    whole = jnp.exp(SUB * keep_log[...])
    for b in range(gain.shape[0]):
        column = jnp.broadcast_to(inverse[b : b + 1, :], (BLOCK, BLOCK)).T
        gain_scale[block(b), :] = column
        for h in range(BLOCK // SUB):
            s = b * (BLOCK // SUB) + h
            last = column[(h + 1) * SUB - 1 : (h + 1) * SUB, :]
            lanes = jnp.concatenate([1.0 / last] * (ends.shape[1] // BLOCK), axis=1)
            ends[s : s + 1, :] = whole * lanes


def halo_kernel(signal, halo):
    halo[...] = signal[signal.shape[0] - halo.shape[0] :, :]


def energy_of(pair, window):
    both = dot(pair, window)
    real, imag = both[:BLOCK], both[BLOCK:]
    return (real * real + imag * imag).astype(jnp.bfloat16)


def inverse_decay(scale, gain_scale):
    cols = scale.shape[1]
    lanes = jnp.concatenate([gain_scale] * (cols // 128), axis=1)
    return jnp.concatenate([scale] * (BLOCK // SUB), axis=0) * lanes


def scaled_energy(energy, rate, scale, gain_scale):
    return energy.astype(jnp.float32) * (inverse_decay(scale, gain_scale) * rate)


def last_sums(scaled):
    return [
        jnp.sum(scaled[h * SUB : (h + 1) * SUB, :], axis=0, keepdims=True)
        for h in range(BLOCK // SUB)
    ]


def block(b, n=1):
    return pl.ds(b * BLOCK, n * BLOCK)


def compose(sums, ends):
    value = jnp.zeros_like(ends[0:1, :])
    decay = jnp.ones_like(value)
    for s, row in sums:
        step = ends[s : s + 1, :]
        value = step * (value + row)
        decay = decay * step
    return jnp.concatenate([decay, value], axis=0)


def main_kernel(
    count, signal, band_m, pair_m, rate, scale, gain_scale, ends, band1, energy, energy_last, tail, band,
    energy_v, sems,
):
    for b in range(1, count):
        band[block(b), :] = dot(band_m[...], signal[block(b - 1, 2), :]).astype(jnp.bfloat16)
    band1[...] = band[block(1), :]
    order = [count - 1, *range(2, count - 1)]
    half = len(order) // 2
    copies = []
    tails = {}

    def send(source, target):
        copy = pltpu.make_async_copy(source, target, sems.at[len(copies)])
        copy.start()
        copies.append(copy)

    for done, b in enumerate(order):
        e = energy_of(pair_m[...], band[block(b - 1, 2), :])
        energy_v[block(b - 2), :] = e
        sums = last_sums(scaled_energy(e, rate[...], scale[...], gain_scale[block(b), :]))
        for h, row in enumerate(sums):
            tails[b * len(sums) + h] = row
        if done == 0:
            send(energy_v.at[block(count - 3), :], energy_last)
        if done == half:
            send(energy_v.at[block(0, half), :], energy.at[block(0, half), :])
    part = block(half, count - 2 - half)
    send(energy_v.at[part, :], energy.at[part, :])
    tail[...] = compose(sorted(tails.items()), ends)
    for copy in copies:
        copy.wait()


def edge_kernel(
    prior, signal, band1, tail, band_m, pair_m, rate, scale, gain_scale, ends,
    energy, totals,
):
    windows = [prior[...], jnp.concatenate([prior[block(1), :], signal[block(0), :]], axis=0)]
    band = [dot(band_m[...], window).astype(jnp.bfloat16) for window in windows] + [band1[...]]
    rows = []
    for b in range(2):
        e = energy_of(pair_m[...], jnp.concatenate([band[b], band[b + 1]], axis=0))
        energy[block(b), :] = e
        rows += last_sums(scaled_energy(e, rate[...], scale[...], gain_scale[block(b), :]))
    first = compose(list(enumerate(rows)), ends)
    decay, value = tail[0:1, :], tail[1:2, :]
    both = jnp.concatenate([decay * first[0:1, :], decay * first[1:2, :] + value], axis=0)
    for k in range(totals.shape[0]):
        totals[k] = both


def carry_kernel(position, totals, start, carry):
    state = start[...]
    for k in range(totals.shape[0]):
        new = totals[k, 0:1, :] * state + totals[k, 1:2, :]
        state = jnp.where(k < position[0], new, state)
    carry[...] = state


def ratio_kernel(
    count, carry, before, head, rest, short_m, sums_m, rate, scale, gain_scale,
    ends, out, buffer, sems,
):
    parts = sems.shape[0]
    each = count // parts
    state = carry[...]

    def energy(b):
        return before[...] if b < 0 else head[block(b), :] if b < 2 else rest[block(b - 2), :]

    sends = []
    for b in range(count):
        current = energy(b)
        inverse = inverse_decay(scale[...], gain_scale[block(b), :])
        scaled = current.astype(jnp.float32) * (inverse * rate[...])
        high = scaled.astype(jnp.bfloat16)
        low = (scaled - high.astype(jnp.float32)).astype(jnp.bfloat16)
        running = dot(sums_m[...], jnp.concatenate([high, low], axis=0))
        window = rest[block(b - 3, 2), :] if b > 2 else jnp.concatenate([energy(b - 1), current], axis=0)
        upper = dot(short_m[...], window) * inverse
        for h in range(BLOCK // SUB):
            at = b * BLOCK + h * SUB
            run = running[h * SUB : (h + 1) * SUB, :]
            buffer[at : at + SUB, :] = upper[h * SUB : (h + 1) * SUB, :] / (run + state)
            s = at // SUB
            state = ends[s : s + 1, :] * (state + run[SUB - 1 : SUB, :])
        if (b + 1) % each == 0:
            c = b // each
            part = block(c * each, each)
            copy = pltpu.make_async_copy(buffer.at[part, :], out.at[part, :], sems.at[c])
            copy.start()
            sends.append(copy)
    for copy in sends:
        copy.wait()


def body(raw, band_taps, real_taps, imag_taps, short_taps, lta_rate, lta_start, gap_gain):
    f32, bf16 = jnp.float32, jnp.bfloat16
    struct = jax.ShapeDtypeStruct
    hbm = lambda x: pltpu.with_memory_space_constraint(x, pltpu.HBM)
    parts, groups = lax.axis_size("chan"), lax.axis_size("tm")
    held, cols = raw.shape[0], raw.shape[1] // parts
    total = held * parts
    count, subs = total // BLOCK, total // SUB
    grouped = call(
        regroup_kernel,
        pltpu.VMEM((parts, held, cols), bf16),
        [HBM],
        out_specs=VMEM,
        scratch=[pltpu.VMEM(raw.shape, bf16), pltpu.SemaphoreType.DMA((3,))],
    )(hbm(raw))
    signal = lax.all_to_all(grouped, "chan", split_axis=0, concat_axis=0, tiled=True)
    signal = signal.reshape(total, cols)

    given = (band_taps, real_taps, imag_taps, short_taps, lta_rate, gap_gain)
    signal, given = lax.optimization_barrier((signal, given))
    band_taps, real_taps, imag_taps, short_taps, lta_rate, gap_gain = given
    taps = [x.reshape(1, BLOCK) for x in (band_taps, real_taps, imag_taps, short_taps)]
    keep_log = jnp.log1p(-(1.0 - (1.0 - lta_rate))).reshape(1, cols)
    rate = lta_rate.reshape(1, cols)
    matrix = struct((BLOCK, 2 * BLOCK), bf16)
    band_m, pair_m, short_m, sums_m, scale, gain_scale, ends = call(
        prepare_kernel,
        [
            matrix,
            struct((2 * BLOCK, 2 * BLOCK), bf16),
            matrix,
            matrix,
            struct((SUB, cols), f32),
            struct((total, 128), f32),
            struct((subs, cols), f32),
        ],
        [VMEM] * 6,
    )(*taps, keep_log, gap_gain.reshape(count, BLOCK))

    halo = call(halo_kernel, pltpu.VMEM((2 * BLOCK, cols), bf16), [VMEM])(signal)
    prior = from_behind(halo, "tm")
    band1, rest, energy_last, tail = call(
        functools.partial(main_kernel, count),
        [
            struct((BLOCK, cols), bf16),
            pltpu.HBM((total - 2 * BLOCK, cols), bf16),
            pltpu.HBM((BLOCK, cols), bf16),
            struct((2, cols), f32),
        ],
        [VMEM] * 7,
        out_specs=[VMEM, HBM, HBM, VMEM],
        scratch=[
            pltpu.VMEM((total, cols), bf16),
            pltpu.VMEM((total - 2 * BLOCK, cols), bf16),
            pltpu.SemaphoreType.DMA((3,)),
        ],
    )(signal, band_m, pair_m, rate, scale, gain_scale, ends)
    energy_before = from_behind(energy_last, "tm")
    head, totals = call(
        edge_kernel,
        [struct((2 * BLOCK, cols), bf16), pltpu.VMEM((groups, 2, cols), f32)],
        [VMEM] * 10,
    )(prior, signal, band1, tail, band_m, pair_m, rate, scale, gain_scale, ends)
    position = lax.axis_index("tm").astype(jnp.int32).reshape(1)
    totals, position, start = lax.optimization_barrier(
        (totals, position, lta_start.reshape(1, cols))
    )
    totals = lax.all_to_all(totals, "tm", split_axis=0, concat_axis=0, tiled=True)
    carry = call(
        carry_kernel, struct((1, cols), f32), [SMEM] + [VMEM] * 2
    )(position, totals, start)
    return call(
        functools.partial(ratio_kernel, count),
        pltpu.HBM((total, cols), f32),
        [VMEM] * 10,
        out_specs=HBM,
        scratch=[pltpu.VMEM((total, cols), f32), pltpu.SemaphoreType.DMA((12,))],
    )(carry, energy_before, head, rest, short_m, sums_m, rate,
      scale, gain_scale, ends)


def solution(mesh):
    return jax.shard_map(
        body,
        mesh=mesh,
        in_specs=(P(("tm", "chan"), None), P(), P(), P(), P(), P("chan"), P("chan"), P("tm")),
        out_specs=P("tm", "chan"),
        check_vma=False,
    )
```
